512 devices in a mesh: tile: 32 (over x, z), pair: 16 (over y, core).
Axes of the slice: x: 4, y: 8, z: 8, core: 2. Of those that a mesh axis runs over, the one named last changes fastest.
Arguments:
- samples: bfloat16 [256, 512, 1024], P('tile', 'pair'), may hold values from -48 to 48
- pair_list: int32 [1024, 2], P('tile'), may hold values from 0 to 255, as said below
- taper_bins: int32 [1024], P(('tile', 'pair')), may hold values from 0 to 7
Outputs:
- covariance: bfloat16 [1024, 1024, 1024], P(('tile', 'pair'))
The draws below stay inside these ranges and needn't reach their ends.
Inputs may be any that keep to these rules, and one draw needn't show every extreme that they name: `pair_list`: pairs are listed by groups of 32 rows; the first tile of every pair of group k is one of tiles k * 8 to (k + 1) * 8 - 1. The second tile lies within 2 tiles of the first, counted cyclically around the band of 256 tiles; in every group some pair reaches 2 tiles down from the group's first tile and some 2 tiles up from its last.
All inputs are finite; a program needn't handle non-finite values.
Results may differ from the reference program's by a relative error of at most 0.0053.
Values may be sent and summed in bfloat16 or wider, within the bound.
A program may use at most 64 MiB of HBM per device.

```python
import jax
import jax.numpy as jnp
from jax import lax

PIX = 1024
REACH = 2
NBINS = 8
TILE_DEV = 8
PAIR_DEV = 2
TILES = 256
SAMPLES = 512
PAIRS = 1024
N_PAIR = 16


def draw_samples(key, part):
    key = jax.random.fold_in(key, 1)
    subkeys = jax.random.split(key, 4)
    base_map = jax.random.uniform(subkeys[0], (TILES, 1, PIX), jnp.float32, -8.0, 8.0)
    amplitude = jnp.exp(jax.random.uniform(subkeys[1], (TILES, 1, PIX), jnp.float32, jnp.log(0.3), jnp.log(3.0)))
    own_noise = jnp.clip(jax.random.normal(subkeys[2], (TILES, SAMPLES, PIX), jnp.float32), -5.0, 5.0)
    shared_noise = jnp.clip(jax.random.normal(subkeys[3], (1, SAMPLES, PIX), jnp.float32), -5.0, 5.0)
    values = base_map + amplitude * (own_noise + 0.7 * shared_noise)
    return values.astype(jnp.bfloat16)


def draw_pair_list(key, part):
    key = jax.random.fold_in(key, 2)
    subkeys = jax.random.split(key, 2)
    group_rows = PAIR_DEV * N_PAIR
    row_index = jnp.arange(PAIRS, dtype=jnp.int32)
    group_index = row_index // group_rows
    slot_index = row_index % group_rows
    first_pick = jax.random.randint(subkeys[0], (PAIRS,), 0, TILE_DEV, dtype=jnp.int32)
    offset_pick = jax.random.randint(subkeys[1], (PAIRS,), -REACH, REACH + 1, dtype=jnp.int32)
    first_pick = jnp.where(slot_index == 0, 0, jnp.where(slot_index == 1, TILE_DEV - 1, first_pick))
    offset_pick = jnp.where(slot_index == 0, -REACH, jnp.where(slot_index == 1, REACH, offset_pick))
    first_tile = group_index * TILE_DEV + first_pick
    second_tile = (first_tile + offset_pick + TILES) % TILES
    return jnp.stack([first_tile, second_tile], axis=1).astype(jnp.int32)


def with_ends(values, key, least, largest):
    dims = values.shape
    index_at = [jax.random.randint(jax.random.fold_in(key, axis), (), 0, dims[axis]) for axis in range(len(dims))]
    values = values.at[tuple(index_at)].set(least)
    longest = dims.index(max(dims))
    index_at[longest] = (index_at[longest] + 1) % dims[longest]
    return values.at[tuple(index_at)].set(largest)


def setup_inputs(seed: int = 0) -> dict:
    seeds = jax.random.split(jax.random.key(seed), 4)
    return {
        "samples": draw_samples(jax.random.fold_in(seeds[3], 71), 0),
        "pair_list": draw_pair_list(jax.random.fold_in(seeds[3], 71), 0),
        "taper_bins": with_ends(jax.random.randint(seeds[2], (PAIRS,), 0, NBINS), jax.random.fold_in(seeds[2], 1), 0, NBINS - 1).astype(jnp.int32),
    }


def reference(samples, pair_list, taper_bins):
    tile_mean = jnp.sum(samples, axis=1, dtype=jnp.float32) / SAMPLES
    centered = (samples.astype(jnp.float32) - tile_mean[:, None, :]).astype(jnp.bfloat16)
    taper_weight = 1.0 - taper_bins.astype(jnp.float32) / NBINS
    factor = taper_weight / jnp.float32(SAMPLES - 1)

    def one_block(pair_index):
        left_rows = centered[pair_list[pair_index, 0]]
        right_rows = centered[pair_list[pair_index, 1]]
        gram_sum = jnp.dot(left_rows.T, right_rows, preferred_element_type=jnp.float32)
        return (gram_sum * factor[pair_index]).astype(jnp.bfloat16)

    return lax.map(one_block, jnp.arange(PAIRS, dtype=jnp.int32))
```

```python
import functools

import jax
import jax.numpy as jnp
from jax import lax
from jax.experimental import pallas as pl
from jax.experimental.pallas import tpu as pltpu
from jax.sharding import PartitionSpec as P

REACH = 2
NBINS = 8
MESH = pl.DeviceIdType.MESH

INNER = slice(0, 4)
ENDS = slice(4, 8)
LAST = slice(4, 6)
FIRST = slice(6, 8)
FROM_PREV = slice(8, 10)
FROM_NEXT = slice(10, 12)
HALO = slice(8, 12)
SLOTS = 12


def slot_of(tile, start, band):
    rel = lax.rem(tile - start + REACH + band, band)
    rel = jnp.clip(rel, 0, SLOTS - 1)
    return jnp.where(rel < 2, rel + 8, jnp.where(rel < 4, rel + 4, jnp.where(rel < 10, rel - 4, rel)))


def gather_kernel(plan, pair_ref, samples_ref, acc_ref, last_ref, sum_ref, *scratch):
    tiles, chips, steps, rows, pixels, per_device = plan
    chunks = 2 * steps + 1
    mine, theirs = scratch[:chunks], scratch[chunks : 2 * chunks]
    u_ref, shift_ref, send_sem, recv_sem, local_sem = scratch[2 * chunks :]
    half = rows // 2
    right_way = [0] + [2 * s - 1 for s in range(1, steps + 1)]
    left_way = [0] + [2 * s for s in range(1, steps + 1)]

    t, p = lax.axis_index("tile"), lax.axis_index("pair")
    group = 2 * chips
    above, below = (lax.rem(t + 1, tiles), p), (lax.rem(t + tiles - 1, tiles), p)
    right, left = (t, lax.rem(p + 2, group)), (t, lax.rem(p + group - 2, group))
    other = (t, p + 1 - 2 * lax.rem(p, 2))

    count = [0]
    sent = []

    def send(src, dst, device):
        k = count[0]
        count[0] += 1
        copy = pltpu.make_async_remote_copy(
            src_ref=src, dst_ref=dst, send_sem=send_sem.at[k], recv_sem=recv_sem.at[k],
            device_id=device, device_id_type=MESH,
        )
        copy.start()
        sent.append(copy)
        return copy

    fills = []
    for k, (lo, hi, slots) in enumerate(((0, 2, FIRST), (6, 8, LAST), (2, 6, INNER))):
        fill = pltpu.make_async_copy(samples_ref.at[lo:hi], mine[0].at[slots], local_sem.at[k])
        fill.start()
        fills.append(fill)
    barrier = pltpu.get_barrier_semaphore()
    for device in (right, left, above, below, other):
        pl.semaphore_signal(barrier, inc=1, device_id=device, device_id_type=MESH)
    pl.semaphore_wait(barrier, 5)
    for fill in fills:
        fill.wait()

    def forward(step, part):
        if step == steps:
            return (None, None)
        r, l = right_way[step], left_way[step]
        r2, l2 = right_way[step + 1], left_way[step + 1]
        if step + 1 == steps:
            return (
                send(mine[r].at[part, 0:half], mine[r2].at[part], right),
                send(mine[l].at[part, half:rows], mine[l2].at[part], left),
            )
        return (
            send(mine[r].at[part], mine[r2].at[part], right),
            send(mine[l].at[part], mine[l2].at[part], left),
        )

    def ends_out(chunk):
        return (
            send(mine[chunk].at[LAST], mine[chunk].at[FROM_PREV], above),
            send(mine[chunk].at[FIRST], mine[chunk].at[FROM_NEXT], below),
        )

    def across(chunk, part):
        return send(mine[chunk].at[part], theirs[chunk].at[part], other)

    def of_step(step):
        return [0] if step == 0 else [right_way[step], left_way[step]]

    start, band = t * 8, tiles * 8

    def load(step, put):
        for q in range(per_device):
            for side in range(2):
                slot = slot_of(pair_ref[p * per_device + q, side], start, band)
                row = 0
                for chunk in of_step(step):
                    for held in (mine[chunk], theirs[chunk]):
                        put(q, side, row, held[slot].astype(jnp.float32))
                        row += held.shape[1]

    def work(step):
        depth = sum(2 * mine[chunk].shape[1] for chunk in of_step(step))
        if step == 0:
            totals = {}

            def add(q, side, row, values):
                total = jnp.sum(values, axis=0, keepdims=True)
                totals[q, side] = total if row == 0 else totals[q, side] + total

            load(0, add)
            for (q, side), total in totals.items():
                shift_ref[2 * q + side] = total * (1.0 / depth)
        final = step == steps
        sums = {}

        def put(q, side, row, values):
            u = (values - shift_ref[2 * q + side]).astype(jnp.bfloat16)
            into = last_ref if final else u_ref
            into[2 * q + side, pl.ds(row, values.shape[0]), :] = u
            total = jnp.sum(u.astype(jnp.float32), axis=0, keepdims=True)
            sums[q, side] = total if row == 0 else sums[q, side] + total

        load(step, put)
        for (q, side), total in sums.items():
            k = 2 * q + side
            sum_ref[k] = total if step == 0 else sum_ref[k] + total
        if final:
            return
        block = min(256, pixels)
        per_pair = pixels // block

        def body(i, _):
            q, m = lax.div(i, per_pair), pl.multiple_of(lax.rem(i, per_pair) * block, block)
            gram = lax.dot_general(
                u_ref[2 * q, 0:depth, pl.ds(m, block)], u_ref[2 * q + 1, 0:depth, :],
                (((0,), (0,)), ((), ())), preferred_element_type=jnp.float32,
            )
            if step == 0:
                acc_ref[q, pl.ds(m, block), :] = gram
            else:
                acc_ref[q, pl.ds(m, block), :] += gram
            return 0

        lax.fori_loop(0, per_device * per_pair, body, 0)

    ring = {}
    halos = {}
    cross = {}
    ring[0, 0] = forward(0, ENDS)
    halos[0] = ends_out(0)
    ring[0, 1] = forward(0, INNER)
    cross[0] = [across(0, ENDS), across(0, INNER)]

    def halo_across(step):
        for chunk in of_step(step):
            for copy in halos[chunk]:
                copy.wait_recv()
            cross[chunk].append(across(chunk, HALO))

    def arrive(step, part, index):
        for chunk, copy in zip(of_step(step), ring[step - 1, index]):
            copy.wait_recv()
        ring[step, index] = forward(step, part)
        if index == 0:
            for chunk in of_step(step):
                halos[chunk] = ends_out(chunk)
                cross[chunk] = []
        for chunk in of_step(step):
            cross[chunk].append(across(chunk, part))

    def ready(step):
        for chunk in of_step(step):
            for copy in cross[chunk]:
                copy.wait_recv()

    halo_across(0)
    for step in range(1, steps + 1):
        arrive(step, ENDS, 0)
        if step == steps:
            ready(step - 1)
            work(step - 1)
        else:
            halo_across(step)
        arrive(step, INNER, 1)
        if step == steps:
            halo_across(step)
        else:
            ready(step - 1)
            work(step - 1)
    ready(steps)
    work(steps)
    for copy in sent:
        copy.wait_send()


def finish_kernel(plan, bins_ref, acc_ref, last_ref, sum_ref, out_ref, stage, sem):
    samples, pixels, per_device = plan
    block = min(256, pixels)
    copies = []
    for q in range(per_device):
        weight = 1.0 - jnp.full((1, pixels), bins_ref[q], jnp.int32).astype(jnp.float32) / NBINS
        factor = weight / jnp.float32(samples - 1)
        total_a, total_b = sum_ref[2 * q], sum_ref[2 * q + 1] * (1.0 / samples)
        for m in range(0, pixels, block):
            rows = slice(m, m + block)
            gram = acc_ref[q, rows, :] + lax.dot_general(
                last_ref[2 * q, :, rows], last_ref[2 * q + 1], (((0,), (0,)), ((), ())),
                preferred_element_type=jnp.float32,
            )
            column = jnp.transpose(total_a[:, rows])
            stage[q, rows, :] = ((gram - column * total_b) * factor).astype(jnp.bfloat16)
            copy = pltpu.make_async_copy(stage.at[q, rows], out_ref.at[q, rows], sem.at[len(copies)])
            copy.start()
            copies.append(copy)
    for copy in copies:
        copy.wait()


def local(tiles, group, samples, pair_list, taper_bins):
    own_tiles, rows, pixels = samples.shape
    chips = group // 2
    steps = chips // 2
    per_device = taper_bins.shape[0]
    total_rows = rows * group
    plan = (tiles, chips, steps, rows, pixels, per_device)
    chunk_rows = [rows] * (2 * steps - 1) + [rows // 2] * 2
    chunks = [pltpu.VMEM((SLOTS, r, pixels), jnp.bfloat16) for r in chunk_rows]
    n_copies = 2 * 2 * steps + (2 + 3) * len(chunks)
    last_rows = 2 * rows
    acc, last, sums = pl.pallas_call(
        functools.partial(gather_kernel, plan),
        out_shape=(
            pltpu.VMEM((per_device, pixels, pixels), jnp.float32),
            pltpu.VMEM((2 * per_device, last_rows, pixels), jnp.bfloat16),
            pltpu.VMEM((2 * per_device, 1, pixels), jnp.float32),
        ),
        in_specs=[pl.BlockSpec(memory_space=pltpu.SMEM), pl.BlockSpec(memory_space=pl.ANY)],
        out_specs=[pl.BlockSpec(memory_space=pltpu.VMEM)] * 3,
        scratch_shapes=[
            *chunks,
            *chunks,
            pltpu.VMEM((2 * per_device, 4 * rows, pixels), jnp.bfloat16),
            pltpu.VMEM((2 * per_device, 1, pixels), jnp.float32),
            pltpu.SemaphoreType.DMA((n_copies,)),
            pltpu.SemaphoreType.DMA((n_copies,)),
            pltpu.SemaphoreType.DMA((3,)),
        ],
        compiler_params=pltpu.CompilerParams(
            collective_id=0, has_side_effects=True, vmem_limit_bytes=36 * 2**20
        ),
        name="gather_and_sum",
    )(pair_list, samples)
    return pl.pallas_call(
        functools.partial(finish_kernel, (total_rows, pixels, per_device)),
        out_shape=jax.ShapeDtypeStruct((per_device, pixels, pixels), jnp.bfloat16),
        in_specs=[pl.BlockSpec(memory_space=pltpu.SMEM)] + [pl.BlockSpec(memory_space=pltpu.VMEM)] * 3,
        out_specs=pl.BlockSpec(memory_space=pl.ANY),
        scratch_shapes=[
            pltpu.VMEM((per_device, pixels, pixels), jnp.bfloat16),
            pltpu.SemaphoreType.DMA((per_device * max(1, pixels // 256),)),
        ],
        compiler_params=pltpu.CompilerParams(vmem_limit_bytes=36 * 2**20),
        name="finish",
    )(taper_bins, acc, last, sums)


def solution(mesh):
    in_specs = (P("tile", "pair", None), P("tile", None), P(("tile", "pair")))
    out_specs = P(("tile", "pair"), None, None)
    body = functools.partial(local, mesh.shape["tile"], mesh.shape["pair"])
    return jax.shard_map(body, mesh=mesh, in_specs=in_specs, out_specs=out_specs, check_vma=False)
```

```python
import functools

import jax
import jax.numpy as jnp
from jax import lax
from jax.experimental import pallas as pl
from jax.experimental.pallas import tpu as pltpu
from jax.sharding import PartitionSpec as P

REACH = 2
NBINS = 8
LINE = 8
MESH = pl.DeviceIdType.MESH

PARTS = {"c": slice(0, 2), "d": slice(2, 4), "e": slice(4, 8)}
LAST, FIRST = slice(4, 6), slice(6, 8)
FROM_BELOW, FROM_ABOVE = slice(8, 10), slice(10, 12)
SLOTS = 12


def schedule(steps):
    order = ["e0", "u0", "c0", "e1", "d0", "s0", "e2", "v0"]
    for step in range(1, steps):
        order += [f"c{step}", f"d{step}"]
        if step == 1:
            order += ["x0", "w0", "e3", "x1", "w1"]
        else:
            order += [f"x{step}", f"e{step + 2}", f"w{step}"]
    order += [f"c{steps}", f"d{steps}", f"x{steps}", f"w{steps}"]
    return [(o[0], int(o[1:])) for o in order if o[0] != "e" or int(o[1:]) <= steps]


def slot_of(tile, start, band):
    rel = jnp.clip(lax.rem(tile - start + REACH + band, band), 0, SLOTS - 1)
    return jnp.where(rel < 2, rel + 8, jnp.where(rel < 4, rel + 4, jnp.where(rel < 10, rel - 4, rel)))


def gather_kernel(plan, pairs_ref, bins_ref, samples_ref, acc_ref, last_ref, sum_ref, factor_ref, *scratch):
    tiles, chips, steps, rows, pixels, per_device = plan
    chunks = 2 * steps + 1
    mine, theirs = scratch[:chunks], scratch[chunks : 2 * chunks]
    u_ref, shift_ref, pairs, bins, send_sem, recv_sem, local_sem, ready_sem = scratch[2 * chunks :]
    half = rows // 2

    def of_step(step):
        return [0] if step == 0 else [2 * step - 1, 2 * step]

    t, p = lax.axis_index("tile"), lax.axis_index("pair")
    group = 2 * chips
    core = lax.rem(p, 2)
    above, below = (lax.rem(t + 1, tiles), p), (lax.rem(t + tiles - 1, tiles), p)
    right, left = (t, lax.rem(p + 2, group)), (t, lax.rem(p + group - 2, group))
    other = (t, p + 1 - 2 * core)

    turned_below = lax.rem(t, LINE) == 0
    turned_above = lax.rem(lax.rem(t + 1, tiles), LINE) == 0
    first_core = core == 0

    def greet(sem, device):
        pl.semaphore_signal(sem, inc=1, device_id=device, device_id_type=MESH)

    fills = {}
    for k, (part, lo, hi) in enumerate((("e", 6, 8), ("e", 0, 2), ("c", 2, 4), ("d", 4, 6))):
        slots = LAST if k == 0 else FIRST if k == 1 else PARTS[part]
        fill = pltpu.make_async_copy(samples_ref.at[lo:hi], mine[0].at[slots], local_sem.at[k])
        fill.start()
        fills.setdefault(part, []).append(fill)
    scalars = [
        pltpu.make_async_copy(pairs_ref, pairs, local_sem.at[4]),
        pltpu.make_async_copy(bins_ref, bins, local_sem.at[5]),
    ]
    for copy in scalars:
        copy.start()

    barrier = pltpu.get_barrier_semaphore()
    greet(barrier, right)
    greet(barrier, left)
    pl.when(jnp.logical_not(first_core))(lambda: greet(barrier, other))
    pl.when(jnp.logical_not(turned_above))(lambda: greet(barrier, above))
    pl.when(turned_below)(lambda: greet(barrier, below))
    pl.semaphore_wait(
        barrier,
        2 + first_core.astype(jnp.int32) + turned_above.astype(jnp.int32)
        + jnp.logical_not(turned_below).astype(jnp.int32),
    )

    count = [0]
    sent = []

    def send(src, dst, device):
        k = count[0]
        count[0] += 1
        copy = pltpu.make_async_remote_copy(
            src_ref=src, dst_ref=dst, send_sem=send_sem.at[k], recv_sem=recv_sem.at[k],
            device_id=device, device_id_type=MESH,
        )
        copy.start()
        sent.append(copy)
        return copy

    ring = {}
    halos = {c: [] for c in range(chunks)}
    cross = {c: [] for c in range(chunks)}
    later = {"s": [], "u": [], "v": []}
    opened = set()

    def when_open(gate, act):
        if gate in opened:
            act()
        else:
            later[gate].append(act)

    def forward(step, part):
        here, there = of_step(step) if step else [0, 0], of_step(step + 1)
        cut = (slice(0, half), slice(half, rows)) if step + 1 == steps else (slice(0, rows),) * 2
        return [
            send(mine[here[k]].at[PARTS[part], cut[k]], mine[there[k]].at[PARTS[part]], (right, left)[k])
            for k in range(2)
        ]

    def arrive(part, step):
        if step == 0:
            for fill in fills[part]:
                fill.wait()
        else:
            for copy in ring[step - 1, part]:
                copy.wait_recv()
        if step < steps:
            ring[step, part] = forward(step, part)

        def to_neighbour(chunk, own, slots, device):
            halos[chunk].append(send(mine[chunk].at[own], mine[chunk].at[slots], device))

        for chunk in of_step(step):
            if part == "e":
                when_open("u", functools.partial(to_neighbour, chunk, LAST, FROM_BELOW, above))
                when_open("v", functools.partial(to_neighbour, chunk, FIRST, FROM_ABOVE, below))
            when_open("s", functools.partial(across, chunk, PARTS[part]))

    def across(chunk, slots):
        cross[chunk].append(send(mine[chunk].at[slots], theirs[chunk].at[slots], other))

    def open_gate(gate):
        if gate == "s":
            pl.when(jnp.logical_not(first_core))(lambda: pl.semaphore_wait(ready_sem.at[0], 1))
        elif gate == "u":
            pl.when(jnp.logical_not(turned_above))(lambda: pl.semaphore_wait(ready_sem.at[1], 1))
        else:
            pl.when(turned_below)(lambda: pl.semaphore_wait(ready_sem.at[2], 1))
        opened.add(gate)
        for act in later[gate]:
            act()

    start, band = t * 8, tiles * 8

    def load(step, put):
        for q in range(per_device):
            for side in range(2):
                slot = slot_of(pairs[side, p * per_device + q], start, band)
                row = 0
                for chunk in of_step(step):
                    for held in (mine[chunk], theirs[chunk]):
                        put(q, side, row, held[slot].astype(jnp.float32))
                        row += held.shape[1]

    def work(step):
        for chunk in of_step(step):
            for copy in cross[chunk]:
                copy.wait_recv()
        depth = sum(2 * mine[chunk].shape[1] for chunk in of_step(step))
        if step == 0:
            for copy in scalars:
                copy.wait()
            for q in range(per_device):
                weight = 1.0 - jnp.full((1, pixels), bins[0, q], jnp.int32).astype(jnp.float32) / NBINS
                factor_ref[q] = weight / jnp.float32(rows * group - 1)
            totals = {}

            def add(q, side, row, values):
                total = jnp.sum(values, axis=0, keepdims=True)
                totals[q, side] = total if row == 0 else totals[q, side] + total

            load(0, add)
            for (q, side), total in totals.items():
                shift_ref[2 * q + side] = (total * (1.0 / depth)).astype(jnp.bfloat16).astype(jnp.float32)
        final = step == steps
        sums = {}

        def put(q, side, row, values):
            u = (values - shift_ref[2 * q + side]).astype(jnp.bfloat16)
            into = last_ref if final else u_ref
            into[2 * q + side, pl.ds(row, values.shape[0]), :] = u
            total = jnp.sum(u.astype(jnp.float32), axis=0, keepdims=True)
            sums[q, side] = total if row == 0 else sums[q, side] + total

        load(step, put)
        for (q, side), total in sums.items():
            k = 2 * q + side
            sum_ref[k] = total if step == 0 else sum_ref[k] + total
        if final:
            return
        block = min(256, pixels)
        per_pair = pixels // block

        def body(i, _):
            q, m = lax.div(i, per_pair), pl.multiple_of(lax.rem(i, per_pair) * block, block)
            gram = lax.dot_general(
                u_ref[2 * q, 0:depth, pl.ds(m, block)], u_ref[2 * q + 1, 0:depth, :],
                (((0,), (0,)), ((), ())), preferred_element_type=jnp.float32,
            )
            if step == 0:
                acc_ref[q, pl.ds(m, block), :] = gram
            else:
                acc_ref[q, pl.ds(m, block), :] += gram
            return 0

        lax.fori_loop(0, per_device * per_pair, body, 0)

    first = True
    for what, step in schedule(steps):
        if what in PARTS:
            arrive(what, step)
        elif what == "x":
            for chunk in of_step(step):
                for copy in halos[chunk]:
                    copy.wait_recv()
                across(chunk, slice(FROM_BELOW.start, FROM_ABOVE.stop))
        elif what == "w":
            work(step)
        else:
            open_gate(what)
        if first:
            pl.when(first_core)(lambda: greet(ready_sem.at[0], other))
            pl.when(jnp.logical_not(turned_below))(lambda: greet(ready_sem.at[1], below))
            pl.when(turned_above)(lambda: greet(ready_sem.at[2], above))
            first = False
    for copy in sent:
        copy.wait_send()


def finish_kernel(plan, acc_ref, last_ref, sum_ref, factor_ref, out_ref, stage, sem):
    samples, pixels, per_device = plan
    block = min(256, pixels)
    copies = []
    for q in range(per_device):
        factor = factor_ref[q]
        total_a, total_b = sum_ref[2 * q], sum_ref[2 * q + 1] * (1.0 / samples)
        for m in range(0, pixels, block):
            rows = slice(m, m + block)
            gram = acc_ref[q, rows, :] + lax.dot_general(
                last_ref[2 * q, :, rows], last_ref[2 * q + 1], (((0,), (0,)), ((), ())),
                preferred_element_type=jnp.float32,
            )
            column = jnp.transpose(total_a[:, rows])
            stage[q, rows, :] = ((gram - column * total_b) * factor).astype(jnp.bfloat16)
            copy = pltpu.make_async_copy(stage.at[q, rows], out_ref.at[q, rows], sem.at[len(copies)])
            copy.start()
            copies.append(copy)
    for copy in copies:
        copy.wait()


def local(tiles, group, samples, pair_list, taper_bins):
    own_tiles, rows, pixels = samples.shape
    chips = group // 2
    steps = chips // 2
    per_device = taper_bins.shape[0]
    total_rows = rows * group
    plan = (tiles, chips, steps, rows, pixels, per_device)
    chunk_rows = [rows] * (2 * steps - 1) + [rows // 2] * 2
    chunks = [pltpu.VMEM((SLOTS, r, pixels), jnp.bfloat16) for r in chunk_rows]
    n_copies = 2 * 3 * steps + (2 + 4) * len(chunks)
    last_rows = 2 * rows
    acc, last, sums, factor = pl.pallas_call(
        functools.partial(gather_kernel, plan),
        out_shape=(
            pltpu.VMEM((per_device, pixels, pixels), jnp.float32),
            pltpu.VMEM((2 * per_device, last_rows, pixels), jnp.bfloat16),
            pltpu.VMEM((2 * per_device, 1, pixels), jnp.float32),
            pltpu.VMEM((per_device, 1, pixels), jnp.float32),
        ),
        in_specs=[pl.BlockSpec(memory_space=pl.ANY)] * 3,
        out_specs=[pl.BlockSpec(memory_space=pltpu.VMEM)] * 4,
        scratch_shapes=[
            *chunks,
            *chunks,
            pltpu.VMEM((2 * per_device, 4 * rows, pixels), jnp.bfloat16),
            pltpu.VMEM((2 * per_device, 1, pixels), jnp.float32),
            pltpu.SMEM((2, pair_list.shape[0]), jnp.int32),
            pltpu.SMEM((1, per_device), jnp.int32),
            pltpu.SemaphoreType.DMA((n_copies,)),
            pltpu.SemaphoreType.DMA((n_copies,)),
            pltpu.SemaphoreType.DMA((6,)),
            pltpu.SemaphoreType.REGULAR((3,)),
        ],
        compiler_params=pltpu.CompilerParams(
            collective_id=0, has_side_effects=True, vmem_limit_bytes=36 * 2**20
        ),
        name="gather_and_sum",
    )(*(pltpu.with_memory_space_constraint(v, pltpu.HBM) for v in (pair_list.T, taper_bins.reshape(1, -1), samples)))
    return pl.pallas_call(
        functools.partial(finish_kernel, (total_rows, pixels, per_device)),
        out_shape=jax.ShapeDtypeStruct((per_device, pixels, pixels), jnp.bfloat16),
        in_specs=[pl.BlockSpec(memory_space=pltpu.VMEM)] * 4,
        out_specs=pl.BlockSpec(memory_space=pl.ANY),
        scratch_shapes=[
            pltpu.VMEM((per_device, pixels, pixels), jnp.bfloat16),
            pltpu.SemaphoreType.DMA((per_device * max(1, pixels // 256),)),
        ],
        compiler_params=pltpu.CompilerParams(vmem_limit_bytes=36 * 2**20),
        name="finish",
    )(acc, last, sums, factor)


def solution(mesh):
    in_specs = (P("tile", "pair", None), P("tile", None), P(("tile", "pair")))
    out_specs = P(("tile", "pair"), None, None)
    body = functools.partial(local, mesh.shape["tile"], mesh.shape["pair"])
    return jax.shard_map(body, mesh=mesh, in_specs=in_specs, out_specs=out_specs, check_vma=False)
```

```python
import functools

import jax
import jax.numpy as jnp
from jax import lax
from jax.experimental import pallas as pl
from jax.experimental.pallas import tpu as pltpu
from jax.sharding import PartitionSpec as P

REACH = 2
NBINS = 8
LINE = 8
MESH = pl.DeviceIdType.MESH

INNER, ENDS, HALO = slice(0, 4), slice(4, 8), slice(8, 12)
LAST, FIRST = 4, 6
FROM_BELOW, FROM_ABOVE = 8, 10
SLOTS = 12
PIECES = 4
SPLIT_ROWS = 16


def schedule(steps):
    if steps == 4:
        text = (
            "p0 q0 i0 p1", "u0 q1 s0 p2", "i1 v0 x0 p3", "w0 q2 x1 i2", "p4 w1 A0 A1", "q3 A2 x2 A3",
            "w2 i3 x3 B0", "B1 B2 q4 w3", "B3 i4 x4 w4",
        )
    else:
        text = ("p0 q0 i0 p1", "u0 q1 s0 i1", "v0 x0 p2 w0", "A0 A1 A2 A3", "q2 x1 i2 x2", "w1 w2")
    return [(o[0], int(o[1:])) for line in text for o in line.split()]


def slot_of(tile, start, band):
    rel = jnp.clip(lax.rem(tile - start + REACH + band, band), 0, SLOTS - 1)
    return jnp.where(rel < 2, rel + 8, jnp.where(rel < 4, rel + 4, jnp.where(rel < 10, rel - 4, rel)))


def gather_kernel(plan, early, pairs_ref, bins_ref, samples_ref, acc_ref, last_ref, factor_ref, *scratch):
    tiles, chips, steps, rows, pixels, per_device = plan
    chunks = 2 * steps + 1
    mine, theirs = scratch[:chunks], scratch[chunks : 2 * chunks]
    sum_ref, u_ref, shift_ref, pairs, bins, send_sem, recv_sem, halo_send, halo_recv, local_sem, ready_sem = scratch[2 * chunks :]
    half = rows // 2

    def of_step(step):
        return [0] if step == 0 else [2 * step - 1, 2 * step]

    t, p = lax.axis_index("tile"), lax.axis_index("pair")
    group = 2 * chips
    core = lax.rem(p, 2)
    above, below = (lax.rem(t + 1, tiles), p), (lax.rem(t + tiles - 1, tiles), p)
    right, left = (t, lax.rem(p + 2, group)), (t, lax.rem(p + group - 2, group))
    other = (t, p + 1 - 2 * core)

    turned_below = lax.rem(t, LINE) == 0
    turned_above = lax.rem(lax.rem(t + 1, tiles), LINE) == 0
    first_core = core == 0

    lead = jnp.where(turned_above, LAST, FIRST)
    ends = {
        "p": (lead, jnp.where(turned_above, FROM_BELOW, FROM_ABOVE), turned_above),
        "q": (LAST + FIRST - lead, jnp.where(turned_above, FROM_ABOVE, FROM_BELOW), jnp.logical_not(turned_above)),
    }
    part_slots = {"p": pl.ds(ends["p"][0], 2), "q": pl.ds(ends["q"][0], 2), "i": INNER}

    def greet(sem, device):
        pl.semaphore_signal(sem, inc=1, device_id=device, device_id_type=MESH)

    fills = {}
    for k, (part, lo, hi) in enumerate((("p", 6, 8), ("p", 0, 2), ("i", 2, 6))):
        at = (LAST, FIRST, INNER.start)[k]
        fill = pltpu.make_async_copy(samples_ref.at[lo:hi], mine[0].at[at : at + hi - lo], local_sem.at[k])
        fill.start()
        fills.setdefault(part, []).append(fill)
    scalars = [
        pltpu.make_async_copy(pairs_ref, pairs, local_sem.at[3]),
        pltpu.make_async_copy(bins_ref, bins, local_sem.at[4]),
    ]
    for copy in scalars:
        copy.start()

    barrier = pltpu.get_barrier_semaphore()
    greet(barrier, right)
    greet(barrier, left)
    pl.when(jnp.logical_not(first_core))(lambda: greet(barrier, other))
    pl.when(jnp.logical_not(turned_above))(lambda: greet(barrier, above))
    pl.when(turned_below)(lambda: greet(barrier, below))
    pl.semaphore_wait(
        barrier,
        2 + first_core.astype(jnp.int32) + turned_above.astype(jnp.int32)
        + jnp.logical_not(turned_below).astype(jnp.int32),
    )

    count = [0]
    sent = []

    def send(src, dst, device):
        k = count[0]
        count[0] += 1
        copy = pltpu.make_async_remote_copy(
            src_ref=src, dst_ref=dst, send_sem=send_sem.at[k], recv_sem=recv_sem.at[k],
            device_id=device, device_id_type=MESH,
        )
        copy.start()
        sent.append(copy)
        return copy

    ring = {}
    cross = {c: [] for c in range(chunks)}
    later = {"s": [], "u": [], "v": []}
    opened = set()

    def forward(step, part):
        here, there = of_step(step) if step else [0, 0], of_step(step + 1)
        cut = (slice(0, half), slice(half, rows)) if step + 1 == steps else (slice(0, rows),) * 2
        slots = part_slots[part]
        return [
            send(mine[here[k]].at[slots, cut[k]], mine[there[k]].at[slots], (right, left)[k])
            for k in range(2)
        ]

    def halo(chunk, part):
        own, slots, up = ends[part]
        way = 1 - up.astype(jnp.int32)
        to = lax.rem(t + jnp.where(up, 1, tiles - 1), tiles)
        return pltpu.make_async_remote_copy(
            src_ref=mine[chunk].at[pl.ds(own, 2)], dst_ref=mine[chunk].at[pl.ds(slots, 2)],
            send_sem=halo_send.at[chunk, way], recv_sem=halo_recv.at[chunk, way],
            device_id=(to, p), device_id_type=MESH,
        )

    def halos_here(chunk, act):
        for way, (own, slots, device) in enumerate(((LAST, FROM_BELOW, above), (FIRST, FROM_ABOVE, below))):
            act(
                pltpu.make_async_remote_copy(
                    src_ref=mine[chunk].at[own : own + 2], dst_ref=mine[chunk].at[slots : slots + 2],
                    send_sem=halo_send.at[chunk, way], recv_sem=halo_recv.at[chunk, way],
                    device_id=device, device_id_type=MESH,
                )
            )

    def across(chunk, slots):
        if "s" in opened:
            cross[chunk].append(send(mine[chunk].at[slots], theirs[chunk].at[slots], other))
        else:
            later["s"].append((chunk, slots))

    def arrive(part, step):
        if step == 0:
            for fill in fills.get(part, ()):
                fill.wait()
        else:
            for copy in ring[step - 1, part]:
                copy.wait_recv()
        if step < steps:
            ring[step, part] = forward(step, part)
        for chunk in of_step(step):
            if part == "p":
                if "v" in opened:
                    halo(chunk, part).start()
                else:
                    pl.when(jnp.logical_not(turned_below))(lambda: halo(chunk, part).start())
                    later["v"].append(chunk)
            elif part == "q":
                if "u" in opened:
                    halo(chunk, part).start()
                else:
                    later["u"].append(chunk)
                across(chunk, ENDS)
            else:
                across(chunk, INNER)

    def open_gate(gate):
        opened.add(gate)
        if gate == "s":
            pl.when(jnp.logical_not(first_core))(lambda: pl.semaphore_wait(ready_sem.at[0], 1))
            for chunk, slots in later["s"]:
                across(chunk, slots)
        elif gate == "u":
            pl.when(jnp.logical_not(turned_above))(lambda: pl.semaphore_wait(ready_sem.at[1], 1))
            for chunk in later["u"]:
                halo(chunk, "q").start()
        else:

            @pl.when(turned_below)
            def _():
                pl.semaphore_wait(ready_sem.at[2], 1)
                for chunk in later["v"]:
                    halo(chunk, "p").start()

    start, band = t * 8, tiles * 8

    def load(step, put):
        for q in range(per_device):
            for side in range(2):
                slot = slot_of(pairs[side, p * per_device + q], start, band)
                row = 0
                for chunk in of_step(step):
                    for held in (mine[chunk], theirs[chunk]):
                        put(q, side, row, held[slot].astype(jnp.float32))
                        row += held.shape[1]

    def work(step):
        for chunk in of_step(step):
            for copy in cross[chunk]:
                copy.wait_recv()
        depth = sum(2 * mine[chunk].shape[1] for chunk in of_step(step))
        if step == 0:
            for copy in scalars:
                copy.wait()
            for q in range(per_device):
                weight = 1.0 - jnp.full((1, pixels), bins[0, q], jnp.int32).astype(jnp.float32) / NBINS
                factor_ref[q] = weight / jnp.float32(rows * group - 1)
            totals = {}

            def add(q, side, row, values):
                total = jnp.sum(values, axis=0, keepdims=True)
                totals[q, side] = total if row == 0 else totals[q, side] + total

            load(0, add)
            for (q, side), total in totals.items():
                shift_ref[2 * q + side] = (total * (1.0 / depth)).astype(jnp.bfloat16).astype(jnp.float32)
        final = step not in early
        into = last_ref if final else u_ref
        before = [n for n in range(step) if (n in early) == (not final)]
        first_row = sum(2 * mine[chunk].shape[1] for n in before for chunk in of_step(n))
        sums = {}

        def put(q, side, row, values):
            u = (values - shift_ref[2 * q + side]).astype(jnp.bfloat16)
            into[2 * q + side, pl.ds(first_row + row, values.shape[0]), :] = u
            total = jnp.sum(u.astype(jnp.float32), axis=0, keepdims=True)
            sums[q, side] = total if row == 0 else sums[q, side] + total

        load(step, put)
        for (q, side), total in sums.items():
            k = 2 * q + side
            total = total if step == 0 else sum_ref[k] + total
            if step < steps:
                sum_ref[k] = total
            else:
                total = total * (-1.0 / (rows * group)) if side == 0 else total
                high = total.astype(jnp.bfloat16).astype(jnp.float32)
                middle = (total - high).astype(jnp.bfloat16).astype(jnp.float32)
                low = total - high - middle
                row = lax.broadcasted_iota(jnp.int32, (SPLIT_ROWS, pixels), 0)
                is_middle = (row == 5) | (row == (2 if side == 0 else 1))
                is_low = row == (4 if side == 0 else 3)
                parts = jnp.where(row > 5, 0.0, jnp.where(is_middle, middle, jnp.where(is_low, low, high)))
                into[k, pl.ds(first_row + depth, SPLIT_ROWS), :] = parts.astype(jnp.bfloat16)

    def product(which, piece):
        cut = sum(2 * mine[chunk].shape[1] for n in early[:2] for chunk in of_step(n))
        from_rows = slice(0, cut) if which == "A" else slice(cut, u_ref.shape[1])
        block = per_device * pixels // PIECES
        q, m = divmod(piece * block, pixels)
        gram = lax.dot_general(
            u_ref[2 * q, from_rows, m : m + block], u_ref[2 * q + 1, from_rows, :],
            (((0,), (0,)), ((), ())), preferred_element_type=jnp.float32,
        )
        if which == "A":
            acc_ref[q, m : m + block, :] = gram
        else:
            acc_ref[q, m : m + block, :] += gram

    first = True
    for what, step in schedule(steps):
        if what in part_slots:
            arrive(what, step)
        elif what == "x":
            for chunk in of_step(step):
                halos_here(chunk, lambda copy: copy.wait_recv())
                across(chunk, HALO)
        elif what == "w":
            work(step)
        elif what in "AB":
            product(what, step)
        else:
            open_gate(what)
        if first:
            pl.when(first_core)(lambda: greet(ready_sem.at[0], other))
            pl.when(jnp.logical_not(turned_below))(lambda: greet(ready_sem.at[1], below))
            pl.when(turned_above)(lambda: greet(ready_sem.at[2], above))
            first = False
    for copy in sent:
        copy.wait_send()
    for chunk in range(chunks):
        halos_here(chunk, lambda copy: copy.wait_send())


def finish_kernel(acc_ref, last_ref, factor_ref, out_ref, stage, sem):
    per_device, pixels, _ = acc_ref.shape
    block = min(256, pixels)
    copies = []
    for q in range(per_device):
        for m in range(0, pixels, block):
            rows = slice(m, m + block)
            gram = acc_ref[q, rows, :] + lax.dot_general(
                last_ref[2 * q, :, rows], last_ref[2 * q + 1], (((0,), (0,)), ((), ())),
                preferred_element_type=jnp.float32,
            )
            stage[q, rows, :] = (gram * factor_ref[q]).astype(jnp.bfloat16)
            copy = pltpu.make_async_copy(stage.at[q, rows], out_ref.at[q, rows], sem.at[len(copies)])
            copy.start()
            copies.append(copy)
    for copy in copies:
        copy.wait()


def local(tiles, group, samples, pair_list, taper_bins):
    own_tiles, rows, pixels = samples.shape
    chips = group // 2
    steps = chips // 2
    per_device = taper_bins.shape[0]
    plan = (tiles, chips, steps, rows, pixels, per_device)
    chunk_rows = [rows] * (2 * steps - 1) + [rows // 2] * 2
    chunks = [pltpu.VMEM((SLOTS, r, pixels), jnp.bfloat16) for r in chunk_rows]
    n_copies = 2 * 3 * steps + 3 * len(chunks)
    early = list(range(steps - 1))
    early_rows = sum(2 * rows * (1 if n == 0 else 2) for n in early)
    last_rows = 2 * rows * chips - early_rows + SPLIT_ROWS
    acc, last, factor = pl.pallas_call(
        functools.partial(gather_kernel, plan, early),
        out_shape=(
            pltpu.VMEM((per_device, pixels, pixels), jnp.float32),
            pltpu.VMEM((2 * per_device, last_rows, pixels), jnp.bfloat16),
            pltpu.VMEM((per_device, 1, pixels), jnp.float32),
        ),
        in_specs=[pl.BlockSpec(memory_space=pl.ANY)] * 3,
        out_specs=[pl.BlockSpec(memory_space=pltpu.VMEM)] * 3,
        scratch_shapes=[
            *chunks,
            *chunks,
            pltpu.VMEM((2 * per_device, 1, pixels), jnp.float32),
            pltpu.VMEM((2 * per_device, early_rows, pixels), jnp.bfloat16),
            pltpu.VMEM((2 * per_device, 1, pixels), jnp.float32),
            pltpu.SMEM((2, pair_list.shape[0]), jnp.int32),
            pltpu.SMEM((1, per_device), jnp.int32),
            pltpu.SemaphoreType.DMA((n_copies,)),
            pltpu.SemaphoreType.DMA((n_copies,)),
            pltpu.SemaphoreType.DMA((len(chunks), 2)),
            pltpu.SemaphoreType.DMA((len(chunks), 2)),
            pltpu.SemaphoreType.DMA((5,)),
            pltpu.SemaphoreType.REGULAR((3,)),
        ],
        compiler_params=pltpu.CompilerParams(
            collective_id=0, has_side_effects=True, vmem_limit_bytes=36 * 2**20
        ),
        name="gather_and_sum",
    )(*(pltpu.with_memory_space_constraint(v, pltpu.HBM) for v in (pair_list.T, taper_bins.reshape(1, -1), samples)))
    return pl.pallas_call(
        finish_kernel,
        out_shape=jax.ShapeDtypeStruct((per_device, pixels, pixels), jnp.bfloat16),
        in_specs=[pl.BlockSpec(memory_space=pltpu.VMEM)] * 3,
        out_specs=pl.BlockSpec(memory_space=pl.ANY),
        scratch_shapes=[
            pltpu.VMEM((per_device, pixels, pixels), jnp.bfloat16),
            pltpu.SemaphoreType.DMA((per_device * max(1, pixels // 256),)),
        ],
        compiler_params=pltpu.CompilerParams(vmem_limit_bytes=36 * 2**20),
        name="finish",
    )(acc, last, factor)


def solution(mesh):
    in_specs = (P("tile", "pair", None), P("tile", None), P(("tile", "pair")))
    out_specs = P(("tile", "pair"), None, None)
    body = functools.partial(local, mesh.shape["tile"], mesh.shape["pair"])
    return jax.shard_map(body, mesh=mesh, in_specs=in_specs, out_specs=out_specs, check_vma=False)
```

```python
import functools

import jax
import jax.numpy as jnp
from jax import lax
from jax.experimental import pallas as pl
from jax.experimental.pallas import tpu as pltpu
from jax.sharding import PartitionSpec as P

REACH = 2
NBINS = 8
LINE = 8
MESH = pl.DeviceIdType.MESH

INNER, ENDS, HALO = slice(0, 4), slice(4, 8), slice(8, 12)
LAST, FIRST = 4, 6
FROM_BELOW, FROM_ABOVE = 8, 10
SLOTS = 12
PIECES = 4
SPLIT_ROWS = 16


def schedule(steps, bottom):
    if steps != 4:
        text = (
            "p0 q0 i0 p1", "u0 q1 s0 i1", "v0 x0 p2 w0", "A0 A1 A2 A3",
            "q2 x1 w1 x2", "i2 m2 w2 y0", "h0 h1",
        )
    elif bottom:
        text = (
            "p0 q0 i0 p1", "u0 q1 s0 i1", "v0 p2 q2 x0", "i2 x1 w0 p3",
            "w1 q3 A0 A1", "x2 A2 A3 i3", "w2 B0 B1 p4", "x3 q4 B2 B3",
            "w3 x4 i4 m4", "w4 y0 h0 h1", "h2 h3",
        )
    else:
        text = (
            "p0 q0 p1 i0", "u0 s0 p2 q1", "p3 v0 i1 x0", "w0 p4 q2 x1",
            "i2 w1 A0 A1", "q3 x2 A2 A3", "i3 w2 B0 B1", "x3 B2 B3 q4",
            "w3 x4 i4 m4", "w4 y0 h0 h1", "h2 h3",
        )
    return [(o[0], int(o[1:])) for line in text for o in line.split()]


def slot_of(tile, start, band):
    rel = jnp.clip(lax.rem(tile - start + REACH + band, band), 0, SLOTS - 1)
    return jnp.where(rel < 2, rel + 8, jnp.where(rel < 4, rel + 4, jnp.where(rel < 10, rel - 4, rel)))


def gather_kernel(plan, early, pairs_ref, bins_ref, samples_ref, acc_ref, last_ref, factor_ref, *scratch):
    tiles, chips, steps, rows, pixels, per_device = plan
    chunks = 2 * steps + 1
    mine, theirs = scratch[:chunks], scratch[chunks : 2 * chunks]
    sum_ref, u_ref, shift_ref, pairs, bins, send_sem, recv_sem, halo_send, halo_recv, local_sem, ready_sem = scratch[2 * chunks :]
    half = rows // 2

    def of_step(step):
        return [0] if step == 0 else [2 * step - 1, 2 * step]

    t, p = lax.axis_index("tile"), lax.axis_index("pair")
    group = 2 * chips
    core = lax.rem(p, 2)
    above, below = (lax.rem(t + 1, tiles), p), (lax.rem(t + tiles - 1, tiles), p)
    right, left = (t, lax.rem(p + 2, group)), (t, lax.rem(p + group - 2, group))
    other = (t, p + 1 - 2 * core)

    turned_below = lax.rem(t, LINE) == 0
    turned_above = lax.rem(lax.rem(t + 1, tiles), LINE) == 0
    first_core = core == 0

    lead = jnp.where(turned_above, LAST, FIRST)
    ends = {
        "p": (lead, jnp.where(turned_above, FROM_BELOW, FROM_ABOVE), turned_above),
        "q": (LAST + FIRST - lead, jnp.where(turned_above, FROM_ABOVE, FROM_BELOW), jnp.logical_not(turned_above)),
    }
    part_slots = {"p": pl.ds(ends["p"][0], 2), "q": pl.ds(ends["q"][0], 2), "i": INNER}

    def greet(sem, device):
        pl.semaphore_signal(sem, inc=1, device_id=device, device_id_type=MESH)

    barrier = pltpu.get_barrier_semaphore()
    greet(barrier, right)
    greet(barrier, left)
    pl.when(jnp.logical_not(first_core))(lambda: greet(barrier, other))
    pl.when(jnp.logical_not(turned_above))(lambda: greet(barrier, above))
    pl.when(turned_below)(lambda: greet(barrier, below))
    fills = {}
    for k, (part, lo, hi) in enumerate((("p", 6, 8), ("p", 0, 2), ("i", 2, 6))):
        at = (LAST, FIRST, INNER.start)[k]
        fill = pltpu.make_async_copy(samples_ref.at[lo:hi], mine[0].at[at : at + hi - lo], local_sem.at[k])
        fill.start()
        fills.setdefault(part, []).append(fill)
    scalars = [
        pltpu.make_async_copy(pairs_ref, pairs, local_sem.at[3]),
        pltpu.make_async_copy(bins_ref, bins, local_sem.at[4]),
    ]
    for copy in scalars:
        copy.start()

    pl.semaphore_wait(
        barrier,
        2 + first_core.astype(jnp.int32) + turned_above.astype(jnp.int32)
        + jnp.logical_not(turned_below).astype(jnp.int32),
    )

    def run(order):
        count = [0]
        sent = []

        def send(src, dst, device):
            k = count[0]
            count[0] += 1
            copy = pltpu.make_async_remote_copy(
                src_ref=src, dst_ref=dst, send_sem=send_sem.at[k], recv_sem=recv_sem.at[k],
                device_id=device, device_id_type=MESH,
            )
            copy.start()
            sent.append(copy)
            return copy

        ring = {}
        cross = {c: [] for c in range(chunks)}
        later = {"s": [], "u": [], "v": []}
        opened = set()

        def forward(step, part, k):
            here = of_step(step)[k] if step else 0
            there = of_step(step + 1)[k]
            cut = (slice(0, half), slice(half, rows))[k] if step + 1 == steps else slice(0, rows)
            slots = part_slots[part]
            return send(mine[here].at[slots, cut], mine[there].at[slots], (right, left)[k])

        def halo(chunk, part):
            own, slots, up = ends[part]
            way = 1 - up.astype(jnp.int32)
            to = lax.rem(t + jnp.where(up, 1, tiles - 1), tiles)
            return pltpu.make_async_remote_copy(
                src_ref=mine[chunk].at[pl.ds(own, 2)], dst_ref=mine[chunk].at[pl.ds(slots, 2)],
                send_sem=halo_send.at[chunk, way], recv_sem=halo_recv.at[chunk, way],
                device_id=(to, p), device_id_type=MESH,
            )

        def halos_here(chunk, act):
            for way, (own, slots, device) in enumerate(((LAST, FROM_BELOW, above), (FIRST, FROM_ABOVE, below))):
                act(
                    pltpu.make_async_remote_copy(
                        src_ref=mine[chunk].at[own : own + 2], dst_ref=mine[chunk].at[slots : slots + 2],
                        send_sem=halo_send.at[chunk, way], recv_sem=halo_recv.at[chunk, way],
                        device_id=device, device_id_type=MESH,
                    )
                )

        def across(chunk, slots):
            if "s" in opened:
                cross[chunk].append(send(mine[chunk].at[slots], theirs[chunk].at[slots], other))
            else:
                later["s"].append((chunk, slots))

        def arrive(part, step):
            if step == 0:
                for fill in fills.get(part, ()):
                    fill.wait()
            ring[step, part] = []
            for k in range(2):
                if step > 0:
                    ring[step - 1, part][k].wait_recv()
                if step < steps:
                    ring[step, part].append(forward(step, part, k))
            for chunk in of_step(step):
                if part == "p":
                    if "v" in opened:
                        halo(chunk, part).start()
                    else:
                        pl.when(jnp.logical_not(turned_below))(lambda: halo(chunk, part).start())
                        later["v"].append(chunk)
                elif part == "q":
                    if "u" in opened:
                        halo(chunk, part).start()
                    else:
                        later["u"].append(chunk)
                    across(chunk, ENDS)
                else:
                    across(chunk, INNER)

        def open_gate(gate):
            opened.add(gate)
            if gate == "s":
                pl.when(jnp.logical_not(first_core))(lambda: pl.semaphore_wait(ready_sem.at[0], 1))
                for chunk, slots in later["s"]:
                    across(chunk, slots)
            elif gate == "u":
                pl.when(jnp.logical_not(turned_above))(lambda: pl.semaphore_wait(ready_sem.at[1], 1))
                for chunk in later["u"]:
                    halo(chunk, "q").start()
            else:

                @pl.when(turned_below)
                def _():
                    pl.semaphore_wait(ready_sem.at[2], 1)
                    for chunk in later["v"]:
                        halo(chunk, "p").start()

        start, band = t * 8, tiles * 8

        def load(step, put, cores):
            for q in range(per_device):
                for side in range(2):
                    slot = slot_of(pairs[side, p * per_device + q], start, band)
                    row = 0
                    for n, core_chunks in enumerate((mine, theirs)):
                        for chunk in of_step(step):
                            held = core_chunks[chunk]
                            if n in cores:
                                put(q, side, row, held[slot].astype(jnp.float32))
                            row += held.shape[1]

        def work(step, cores=(0, 1)):
            if 1 in cores:
                for chunk in of_step(step):
                    for copy in cross[chunk]:
                        copy.wait_recv()
            depth = sum(2 * mine[chunk].shape[1] for chunk in of_step(step))
            if step == 0:
                for copy in scalars:
                    copy.wait()
                for q in range(per_device):
                    weight = 1.0 - jnp.full((1, pixels), bins[0, q], jnp.int32).astype(jnp.float32) / NBINS
                    factor_ref[q] = weight / jnp.float32(rows * group - 1)
                totals = {}

                def add(q, side, row, values):
                    total = jnp.sum(values, axis=0, keepdims=True)
                    totals[q, side] = total if row == 0 else totals[q, side] + total

                load(0, add, cores)
                for (q, side), total in totals.items():
                    shift_ref[2 * q + side] = (total * (1.0 / depth)).astype(jnp.bfloat16).astype(jnp.float32)
            final = step not in early
            into = last_ref if final else u_ref
            before = [n for n in range(step) if (n in early) == (not final)]
            first_row = sum(2 * mine[chunk].shape[1] for n in before for chunk in of_step(n))
            sums = {}

            def put(q, side, row, values):
                u = (values - shift_ref[2 * q + side]).astype(jnp.bfloat16)
                into[2 * q + side, pl.ds(first_row + row, values.shape[0]), :] = u
                total = jnp.sum(u.astype(jnp.float32), axis=0, keepdims=True)
                sums[q, side] = sums[q, side] + total if (q, side) in sums else total

            load(step, put, cores)
            for (q, side), total in sums.items():
                k = 2 * q + side
                total = total if step == 0 else sum_ref[k] + total
                if step < steps or 1 not in cores:
                    sum_ref[k] = total
                else:
                    total = total * (-1.0 / (rows * group)) if side == 0 else total
                    high = total.astype(jnp.bfloat16).astype(jnp.float32)
                    middle = (total - high).astype(jnp.bfloat16).astype(jnp.float32)
                    low = total - high - middle
                    row = lax.broadcasted_iota(jnp.int32, (SPLIT_ROWS, pixels), 0)
                    is_middle = (row == 5) | (row == (2 if side == 0 else 1))
                    is_low = row == (4 if side == 0 else 3)
                    parts = jnp.where(row > 5, 0.0, jnp.where(is_middle, middle, jnp.where(is_low, low, high)))
                    into[k, pl.ds(first_row + depth, SPLIT_ROWS), :] = parts.astype(jnp.bfloat16)

        state = [0, 0]

        def drain():
            done, mark = state
            for copy in sent[done:mark]:
                copy.wait_send()
            state[:] = mark, len(sent)

        def drain_halos(step):
            for chunk in of_step(step):
                halos_here(chunk, lambda copy: copy.wait_send())

        def product(which, piece):
            cut = sum(2 * mine[chunk].shape[1] for n in early[:2] for chunk in of_step(n))
            from_rows = slice(0, cut) if which == "A" else slice(cut, u_ref.shape[1])
            block = per_device * pixels // PIECES
            q, m = divmod(piece * block, pixels)
            gram = lax.dot_general(
                u_ref[2 * q, from_rows, m : m + block], u_ref[2 * q + 1, from_rows, :],
                (((0,), (0,)), ((), ())), preferred_element_type=jnp.float32,
            )
            if which == "A":
                acc_ref[q, m : m + block, :] = gram
            else:
                acc_ref[q, m : m + block, :] += gram

        first = True
        for what, step in order:
            if what in part_slots:
                arrive(what, step)
            elif what == "x":
                for chunk in of_step(step):
                    halos_here(chunk, lambda copy: copy.wait_recv())
                    across(chunk, HALO)
            elif what == "m":
                work(step, (0,))
            elif what == "w":
                work(step, (1,) if step == steps else (0, 1))
            elif what == "y":
                drain()
            elif what == "h":
                drain_halos(step)
            elif what in "AB":
                product(what, step)
            else:
                open_gate(what)
            if first:
                pl.when(first_core)(lambda: greet(ready_sem.at[0], other))
                pl.when(jnp.logical_not(turned_below))(lambda: greet(ready_sem.at[1], below))
                pl.when(turned_above)(lambda: greet(ready_sem.at[2], above))
                first = False
        drain()
        drain()
        drain_halos(steps)

    pl.when(turned_below)(lambda: run(schedule(steps, True)))
    pl.when(jnp.logical_not(turned_below))(lambda: run(schedule(steps, False)))


def finish_kernel(acc_ref, last_ref, factor_ref, out_ref, stage, sem):
    per_device, pixels, _ = acc_ref.shape
    block = min(256, pixels)
    copies = []
    for q in range(per_device):
        for m in range(0, pixels, block):
            rows = slice(m, m + block)
            gram = acc_ref[q, rows, :] + lax.dot_general(
                last_ref[2 * q, :, rows], last_ref[2 * q + 1], (((0,), (0,)), ((), ())),
                preferred_element_type=jnp.float32,
            )
            stage[q, rows, :] = (gram * factor_ref[q]).astype(jnp.bfloat16)
            copy = pltpu.make_async_copy(stage.at[q, rows], out_ref.at[q, rows], sem.at[len(copies)])
            copy.start()
            copies.append(copy)
    for copy in copies:
        copy.wait()


def local(tiles, group, samples, pair_list, taper_bins):
    own_tiles, rows, pixels = samples.shape
    chips = group // 2
    steps = chips // 2
    per_device = taper_bins.shape[0]
    plan = (tiles, chips, steps, rows, pixels, per_device)
    chunk_rows = [rows] * (2 * steps - 1) + [rows // 2] * 2
    chunks = [pltpu.VMEM((SLOTS, r, pixels), jnp.bfloat16) for r in chunk_rows]
    n_copies = 2 * 3 * steps + 3 * len(chunks)
    early = list(range(steps - 1))
    early_rows = sum(2 * rows * (1 if n == 0 else 2) for n in early)
    last_rows = 2 * rows * chips - early_rows + SPLIT_ROWS
    acc, last, factor = pl.pallas_call(
        functools.partial(gather_kernel, plan, early),
        out_shape=(
            pltpu.VMEM((per_device, pixels, pixels), jnp.float32),
            pltpu.VMEM((2 * per_device, last_rows, pixels), jnp.bfloat16),
            pltpu.VMEM((per_device, 1, pixels), jnp.float32),
        ),
        in_specs=[pl.BlockSpec(memory_space=pl.ANY)] * 3,
        out_specs=[pl.BlockSpec(memory_space=pltpu.VMEM)] * 3,
        scratch_shapes=[
            *chunks,
            *chunks,
            pltpu.VMEM((2 * per_device, 1, pixels), jnp.float32),
            pltpu.VMEM((2 * per_device, early_rows, pixels), jnp.bfloat16),
            pltpu.VMEM((2 * per_device, 1, pixels), jnp.float32),
            pltpu.SMEM((2, pair_list.shape[0]), jnp.int32),
            pltpu.SMEM((1, per_device), jnp.int32),
            pltpu.SemaphoreType.DMA((n_copies,)),
            pltpu.SemaphoreType.DMA((n_copies,)),
            pltpu.SemaphoreType.DMA((len(chunks), 2)),
            pltpu.SemaphoreType.DMA((len(chunks), 2)),
            pltpu.SemaphoreType.DMA((5,)),
            pltpu.SemaphoreType.REGULAR((3,)),
        ],
        compiler_params=pltpu.CompilerParams(
            collective_id=0, has_side_effects=True, vmem_limit_bytes=36 * 2**20
        ),
        name="gather_and_sum",
    )(*(pltpu.with_memory_space_constraint(v, pltpu.HBM) for v in (pair_list.T, taper_bins.reshape(1, -1), samples)))
    return pl.pallas_call(
        finish_kernel,
        out_shape=jax.ShapeDtypeStruct((per_device, pixels, pixels), jnp.bfloat16),
        in_specs=[pl.BlockSpec(memory_space=pltpu.VMEM)] * 3,
        out_specs=pl.BlockSpec(memory_space=pl.ANY),
        scratch_shapes=[
            pltpu.VMEM((per_device, pixels, pixels), jnp.bfloat16),
            pltpu.SemaphoreType.DMA((per_device * max(1, pixels // 256),)),
        ],
        compiler_params=pltpu.CompilerParams(vmem_limit_bytes=36 * 2**20),
        name="finish",
    )(acc, last, factor)


def solution(mesh):
    in_specs = (P("tile", "pair", None), P("tile", None), P(("tile", "pair")))
    out_specs = P(("tile", "pair"), None, None)
    body = functools.partial(local, mesh.shape["tile"], mesh.shape["pair"])
    return jax.shard_map(body, mesh=mesh, in_specs=in_specs, out_specs=out_specs, check_vma=False)
```

```python
import functools

import jax
import jax.numpy as jnp
from jax import lax
from jax.experimental import pallas as pl
from jax.experimental.pallas import tpu as pltpu
from jax.sharding import PartitionSpec as P

REACH = 2
NBINS = 8
LINE = 8
MESH = pl.DeviceIdType.MESH

INNER, ENDS, HALO = slice(0, 4), slice(4, 8), slice(8, 12)
LAST, FIRST = 4, 6
FROM_BELOW, FROM_ABOVE = 8, 10
SLOTS = 12
PIECES = 4
SPLIT_ROWS = 16


def schedule(steps, bottom):
    if steps != 4:
        text = (
            "p0 q0 i0 p1", "u0 q1 s0 i1", "v0 x0 p2 w0", "A0 A1 A2 A3",
            "q2 x1 w1 x2", "i2 m2 w2 y0", "h0 h1",
        )
    elif bottom:
        text = (
            "p0 q0 i0 p1", "u0 q1 s0 i1", "v0 p2 q2 x0", "i2 x1 w0 p3",
            "w1 q3 A0 A1", "x2 A2 A3 i3", "w2 B0 B1 p4", "x3 q4 B2 B3",
            "w3 x4 i4 m4", "w4 y0 h0 h1", "h2 h3",
        )
    else:
        text = (
            "p0 q0 c0 p1", "u0 s0 c1 p2", "q1 p3 d0 v0", "q2 x0 d1 p4",
            "w0 q3 x1 c2", "w1 A0 A1 d2", "q4 x2 A2 A3", "c3 w2 B0 B1",
            "d3 x3 B2 B3", "w3 x4 c4 d4", "m4 w4 y0 h0", "h1 h2 h3",
        )
    return [(o[0], int(o[1:])) for line in text for o in line.split()]


def slot_of(tile, start, band):
    rel = jnp.clip(lax.rem(tile - start + REACH + band, band), 0, SLOTS - 1)
    return jnp.where(rel < 2, rel + 8, jnp.where(rel < 4, rel + 4, jnp.where(rel < 10, rel - 4, rel)))


def gather_kernel(plan, early, pairs_ref, bins_ref, samples_ref, acc_ref, last_ref, factor_ref, *scratch):
    tiles, chips, steps, rows, pixels, per_device = plan
    chunks = 2 * steps + 1
    mine, theirs = scratch[:chunks], scratch[chunks : 2 * chunks]
    sum_ref, u_ref, shift_ref, pairs, bins, send_sem, recv_sem, halo_send, halo_recv, local_sem, ready_sem = scratch[2 * chunks :]
    half = rows // 2

    def of_step(step):
        return [0] if step == 0 else [2 * step - 1, 2 * step]

    t, p = lax.axis_index("tile"), lax.axis_index("pair")
    group = 2 * chips
    core = lax.rem(p, 2)
    above, below = (lax.rem(t + 1, tiles), p), (lax.rem(t + tiles - 1, tiles), p)
    right, left = (t, lax.rem(p + 2, group)), (t, lax.rem(p + group - 2, group))
    other = (t, p + 1 - 2 * core)

    turned_below = lax.rem(t, LINE) == 0
    turned_above = lax.rem(lax.rem(t + 1, tiles), LINE) == 0
    first_core = core == 0

    lead = jnp.where(turned_above, LAST, FIRST)
    ends = {
        "p": (lead, jnp.where(turned_above, FROM_BELOW, FROM_ABOVE), turned_above),
        "q": (LAST + FIRST - lead, jnp.where(turned_above, FROM_ABOVE, FROM_BELOW), jnp.logical_not(turned_above)),
    }
    part_slots = {"p": pl.ds(ends["p"][0], 2), "q": pl.ds(ends["q"][0], 2), "i": INNER, "c": slice(0, 2), "d": slice(2, 4)}

    def greet(sem, device):
        pl.semaphore_signal(sem, inc=1, device_id=device, device_id_type=MESH)

    barrier = pltpu.get_barrier_semaphore()
    greet(barrier, right)
    greet(barrier, left)
    pl.when(jnp.logical_not(first_core))(lambda: greet(barrier, other))
    pl.when(jnp.logical_not(turned_above))(lambda: greet(barrier, above))
    pl.when(turned_below)(lambda: greet(barrier, below))
    fills = {}
    for k, (part, lo, hi) in enumerate((("p", 6, 8), ("p", 0, 2), ("i", 2, 6))):
        at = (LAST, FIRST, INNER.start)[k]
        fill = pltpu.make_async_copy(samples_ref.at[lo:hi], mine[0].at[at : at + hi - lo], local_sem.at[k])
        fill.start()
        fills.setdefault(part, []).append(fill)
    scalars = [
        pltpu.make_async_copy(pairs_ref, pairs, local_sem.at[3]),
        pltpu.make_async_copy(bins_ref, bins, local_sem.at[4]),
    ]
    for copy in scalars:
        copy.start()

    pl.semaphore_wait(
        barrier,
        2 + first_core.astype(jnp.int32) + turned_above.astype(jnp.int32)
        + jnp.logical_not(turned_below).astype(jnp.int32),
    )

    def run(order):
        count = [0]
        sent = []

        def send(src, dst, device):
            k = count[0]
            count[0] += 1
            copy = pltpu.make_async_remote_copy(
                src_ref=src, dst_ref=dst, send_sem=send_sem.at[k], recv_sem=recv_sem.at[k],
                device_id=device, device_id_type=MESH,
            )
            copy.start()
            sent.append(copy)
            return copy

        ring = {}
        cross = {c: [] for c in range(chunks)}
        later = {"s": [], "u": [], "v": []}
        opened = set()

        def forward(step, part, k):
            here = of_step(step)[k] if step else 0
            there = of_step(step + 1)[k]
            cut = (slice(0, half), slice(half, rows))[k] if step + 1 == steps else slice(0, rows)
            slots = part_slots[part]
            return send(mine[here].at[slots, cut], mine[there].at[slots], (right, left)[k])

        def halo(chunk, part):
            own, slots, up = ends[part]
            way = 1 - up.astype(jnp.int32)
            to = lax.rem(t + jnp.where(up, 1, tiles - 1), tiles)
            return pltpu.make_async_remote_copy(
                src_ref=mine[chunk].at[pl.ds(own, 2)], dst_ref=mine[chunk].at[pl.ds(slots, 2)],
                send_sem=halo_send.at[chunk, way], recv_sem=halo_recv.at[chunk, way],
                device_id=(to, p), device_id_type=MESH,
            )

        def halos_here(chunk, act):
            for way, (own, slots, device) in enumerate(((LAST, FROM_BELOW, above), (FIRST, FROM_ABOVE, below))):
                act(
                    pltpu.make_async_remote_copy(
                        src_ref=mine[chunk].at[own : own + 2], dst_ref=mine[chunk].at[slots : slots + 2],
                        send_sem=halo_send.at[chunk, way], recv_sem=halo_recv.at[chunk, way],
                        device_id=device, device_id_type=MESH,
                    )
                )

        def across(chunk, slots):
            if "s" in opened:
                cross[chunk].append(send(mine[chunk].at[slots], theirs[chunk].at[slots], other))
            else:
                later["s"].append((chunk, slots))

        def arrive(part, step):
            if step == 0:
                for fill in fills.get("i" if part == "c" else part, ()):
                    fill.wait()
            ring[step, part] = []
            for k in range(2):
                if step > 0:
                    ring[step - 1, part][k].wait_recv()
                if step < steps:
                    ring[step, part].append(forward(step, part, k))
            for chunk in of_step(step):
                if part == "p":
                    if "v" in opened:
                        halo(chunk, part).start()
                    else:
                        pl.when(jnp.logical_not(turned_below))(lambda: halo(chunk, part).start())
                        later["v"].append(chunk)
                elif part == "q":
                    if "u" in opened:
                        halo(chunk, part).start()
                    else:
                        later["u"].append(chunk)
                    across(chunk, ENDS)
                else:
                    across(chunk, part_slots[part])

        def open_gate(gate):
            opened.add(gate)
            if gate == "s":
                pl.when(jnp.logical_not(first_core))(lambda: pl.semaphore_wait(ready_sem.at[0], 1))
                for chunk, slots in later["s"]:
                    across(chunk, slots)
            elif gate == "u":
                pl.when(jnp.logical_not(turned_above))(lambda: pl.semaphore_wait(ready_sem.at[1], 1))
                for chunk in later["u"]:
                    halo(chunk, "q").start()
            else:

                @pl.when(turned_below)
                def _():
                    pl.semaphore_wait(ready_sem.at[2], 1)
                    for chunk in later["v"]:
                        halo(chunk, "p").start()

        start, band = t * 8, tiles * 8

        def load(step, put, cores):
            for q in range(per_device):
                for side in range(2):
                    slot = slot_of(pairs[side, p * per_device + q], start, band)
                    row = 0
                    for n, core_chunks in enumerate((mine, theirs)):
                        for chunk in of_step(step):
                            held = core_chunks[chunk]
                            if n in cores:
                                put(q, side, row, held[slot].astype(jnp.float32))
                            row += held.shape[1]

        def work(step, cores=(0, 1)):
            if 1 in cores:
                for chunk in of_step(step):
                    for copy in cross[chunk]:
                        copy.wait_recv()
            depth = sum(2 * mine[chunk].shape[1] for chunk in of_step(step))
            if step == 0:
                for copy in scalars:
                    copy.wait()
                for q in range(per_device):
                    weight = 1.0 - jnp.full((1, pixels), bins[0, q], jnp.int32).astype(jnp.float32) / NBINS
                    factor_ref[q] = weight / jnp.float32(rows * group - 1)
                totals = {}

                def add(q, side, row, values):
                    total = jnp.sum(values, axis=0, keepdims=True)
                    totals[q, side] = total if row == 0 else totals[q, side] + total

                load(0, add, cores)
                for (q, side), total in totals.items():
                    shift_ref[2 * q + side] = (total * (1.0 / depth)).astype(jnp.bfloat16).astype(jnp.float32)
            final = step not in early
            into = last_ref if final else u_ref
            before = [n for n in range(step) if (n in early) == (not final)]
            first_row = sum(2 * mine[chunk].shape[1] for n in before for chunk in of_step(n))
            sums = {}

            def put(q, side, row, values):
                u = (values - shift_ref[2 * q + side]).astype(jnp.bfloat16)
                into[2 * q + side, pl.ds(first_row + row, values.shape[0]), :] = u
                total = jnp.sum(u.astype(jnp.float32), axis=0, keepdims=True)
                sums[q, side] = sums[q, side] + total if (q, side) in sums else total

            load(step, put, cores)
            for (q, side), total in sums.items():
                k = 2 * q + side
                total = total if step == 0 else sum_ref[k] + total
                if step < steps or 1 not in cores:
                    sum_ref[k] = total
                else:
                    total = total * (-1.0 / (rows * group)) if side == 0 else total
                    high = total.astype(jnp.bfloat16).astype(jnp.float32)
                    middle = (total - high).astype(jnp.bfloat16).astype(jnp.float32)
                    low = total - high - middle
                    row = lax.broadcasted_iota(jnp.int32, (SPLIT_ROWS, pixels), 0)
                    is_middle = (row == 5) | (row == (2 if side == 0 else 1))
                    is_low = row == (4 if side == 0 else 3)
                    parts = jnp.where(row > 5, 0.0, jnp.where(is_middle, middle, jnp.where(is_low, low, high)))
                    into[k, pl.ds(first_row + depth, SPLIT_ROWS), :] = parts.astype(jnp.bfloat16)

        state = [0, 0]

        def drain():
            done, mark = state
            for copy in sent[done:mark]:
                copy.wait_send()
            state[:] = mark, len(sent)

        def drain_halos(step):
            for chunk in of_step(step):
                halos_here(chunk, lambda copy: copy.wait_send())

        def product(which, piece):
            cut = sum(2 * mine[chunk].shape[1] for n in early[:2] for chunk in of_step(n))
            from_rows = slice(0, cut) if which == "A" else slice(cut, u_ref.shape[1])
            block = per_device * pixels // PIECES
            q, m = divmod(piece * block, pixels)
            gram = lax.dot_general(
                u_ref[2 * q, from_rows, m : m + block], u_ref[2 * q + 1, from_rows, :],
                (((0,), (0,)), ((), ())), preferred_element_type=jnp.float32,
            )
            if which == "A":
                acc_ref[q, m : m + block, :] = gram
            else:
                acc_ref[q, m : m + block, :] += gram

        first = True
        for what, step in order:
            if what in part_slots:
                arrive(what, step)
            elif what == "x":
                for chunk in of_step(step):
                    halos_here(chunk, lambda copy: copy.wait_recv())
                    across(chunk, HALO)
            elif what == "m":
                work(step, (0,))
            elif what == "w":
                work(step, (1,) if step == steps else (0, 1))
            elif what == "y":
                drain()
            elif what == "h":
                drain_halos(step)
            elif what in "AB":
                product(what, step)
            else:
                open_gate(what)
            if first:
                pl.when(first_core)(lambda: greet(ready_sem.at[0], other))
                pl.when(jnp.logical_not(turned_below))(lambda: greet(ready_sem.at[1], below))
                pl.when(turned_above)(lambda: greet(ready_sem.at[2], above))
                first = False
        drain()
        drain()
        drain_halos(steps)

    pl.when(turned_below)(lambda: run(schedule(steps, True)))
    pl.when(jnp.logical_not(turned_below))(lambda: run(schedule(steps, False)))


def finish_kernel(acc_ref, last_ref, factor_ref, out_ref, stage, sem):
    per_device, pixels, _ = acc_ref.shape
    block = min(256, pixels)
    copies = []
    for q in range(per_device):
        for m in range(0, pixels, block):
            rows = slice(m, m + block)
            gram = acc_ref[q, rows, :] + lax.dot_general(
                last_ref[2 * q, :, rows], last_ref[2 * q + 1], (((0,), (0,)), ((), ())),
                preferred_element_type=jnp.float32,
            )
            stage[q, rows, :] = (gram * factor_ref[q]).astype(jnp.bfloat16)
            copy = pltpu.make_async_copy(stage.at[q, rows], out_ref.at[q, rows], sem.at[len(copies)])
            copy.start()
            copies.append(copy)
    for copy in copies:
        copy.wait()


def local(tiles, group, samples, pair_list, taper_bins):
    own_tiles, rows, pixels = samples.shape
    chips = group // 2
    steps = chips // 2
    per_device = taper_bins.shape[0]
    plan = (tiles, chips, steps, rows, pixels, per_device)
    chunk_rows = [rows] * (2 * steps - 1) + [rows // 2] * 2
    chunks = [pltpu.VMEM((SLOTS, r, pixels), jnp.bfloat16) for r in chunk_rows]
    n_copies = 2 * 4 * steps + 4 * len(chunks)
    early = list(range(steps - 1))
    early_rows = sum(2 * rows * (1 if n == 0 else 2) for n in early)
    last_rows = 2 * rows * chips - early_rows + SPLIT_ROWS
    acc, last, factor = pl.pallas_call(
        functools.partial(gather_kernel, plan, early),
        out_shape=(
            pltpu.VMEM((per_device, pixels, pixels), jnp.float32),
            pltpu.VMEM((2 * per_device, last_rows, pixels), jnp.bfloat16),
            pltpu.VMEM((per_device, 1, pixels), jnp.float32),
        ),
        in_specs=[pl.BlockSpec(memory_space=pl.ANY)] * 3,
        out_specs=[pl.BlockSpec(memory_space=pltpu.VMEM)] * 3,
        scratch_shapes=[
            *chunks,
            *chunks,
            pltpu.VMEM((2 * per_device, 1, pixels), jnp.float32),
            pltpu.VMEM((2 * per_device, early_rows, pixels), jnp.bfloat16),
            pltpu.VMEM((2 * per_device, 1, pixels), jnp.float32),
            pltpu.SMEM((2, pair_list.shape[0]), jnp.int32),
            pltpu.SMEM((1, per_device), jnp.int32),
            pltpu.SemaphoreType.DMA((n_copies,)),
            pltpu.SemaphoreType.DMA((n_copies,)),
            pltpu.SemaphoreType.DMA((len(chunks), 2)),
            pltpu.SemaphoreType.DMA((len(chunks), 2)),
            pltpu.SemaphoreType.DMA((5,)),
            pltpu.SemaphoreType.REGULAR((3,)),
        ],
        compiler_params=pltpu.CompilerParams(
            collective_id=0, has_side_effects=True, vmem_limit_bytes=36 * 2**20
        ),
        name="gather_and_sum",
    )(*(pltpu.with_memory_space_constraint(v, pltpu.HBM) for v in (pair_list.T, taper_bins.reshape(1, -1), samples)))
    return pl.pallas_call(
        finish_kernel,
        out_shape=jax.ShapeDtypeStruct((per_device, pixels, pixels), jnp.bfloat16),
        in_specs=[pl.BlockSpec(memory_space=pltpu.VMEM)] * 3,
        out_specs=pl.BlockSpec(memory_space=pl.ANY),
        scratch_shapes=[
            pltpu.VMEM((per_device, pixels, pixels), jnp.bfloat16),
            pltpu.SemaphoreType.DMA((per_device * max(1, pixels // 256),)),
        ],
        compiler_params=pltpu.CompilerParams(vmem_limit_bytes=36 * 2**20),
        name="finish",
    )(acc, last, factor)


def solution(mesh):
    in_specs = (P("tile", "pair", None), P("tile", None), P(("tile", "pair")))
    out_specs = P(("tile", "pair"), None, None)
    body = functools.partial(local, mesh.shape["tile"], mesh.shape["pair"])
    return jax.shard_map(body, mesh=mesh, in_specs=in_specs, out_specs=out_specs, check_vma=False)
```

```python
import functools

import jax
import jax.numpy as jnp
from jax import lax
from jax.experimental import pallas as pl
from jax.experimental.pallas import tpu as pltpu
from jax.sharding import PartitionSpec as P

REACH = 2
NBINS = 8
LINE = 8
MESH = pl.DeviceIdType.MESH

INNER, ENDS, HALO = slice(0, 4), slice(4, 8), slice(8, 12)
LAST, FIRST = 4, 6
FROM_BELOW, FROM_ABOVE = 8, 10
SLOTS = 12
PIECES = 4
SPLIT_ROWS = 16


def schedule(steps, bottom):
    if steps != 4:
        text = (
            "p0 q0 i0 p1", "u0 q1 s0 i1", "v0 x0 p2 w0", "A0 A1 A2 A3",
            "q2 x1 w1 x2", "i2 m2 w2 y0", "h0 h1",
        )
    elif bottom:
        text = (
            "p0 q0 c0 d0", "p1 u0 q1 s0", "c1 d1 v0 p2", "q2 x0 c2 d2",
            "x1 w0 p3 w1", "q3 A0 A1 x2", "A2 A3 c3 d3", "w2 B0 B1 p4",
            "x3 q4 B2 B3", "w3 x4 c4 d4", "m4 w4 y0 h0", "h1 h2 h3",
        )
    else:
        text = (
            "p0 q0 c0 p1", "u0 s0 c1 p2", "q1 p3 d0 v0", "q2 x0 d1 p4",
            "w0 q3 x1 c2", "w1 A0 A1 d2", "q4 x2 A2 A3", "c3 w2 B0 B1",
            "d3 x3 B2 B3", "w3 x4 c4 d4", "m4 w4 y0 h0", "h1 h2 h3",
        )
    return [(o[0], int(o[1:])) for line in text for o in line.split()]


def slot_of(tile, start, band):
    rel = jnp.clip(lax.rem(tile - start + REACH + band, band), 0, SLOTS - 1)
    return jnp.where(rel < 2, rel + 8, jnp.where(rel < 4, rel + 4, jnp.where(rel < 10, rel - 4, rel)))


def gather_kernel(plan, early, pairs_ref, bins_ref, samples_ref, acc_ref, last_ref, factor_ref, *scratch):
    tiles, chips, steps, rows, pixels, per_device = plan
    chunks = 2 * steps + 1
    mine, theirs = scratch[:chunks], scratch[chunks : 2 * chunks]
    sum_ref, u_ref, shift_ref, pairs, bins, send_sem, recv_sem, halo_send, halo_recv, local_sem, ready_sem = scratch[2 * chunks :]
    half = rows // 2

    def of_step(step):
        return [0] if step == 0 else [2 * step - 1, 2 * step]

    t, p = lax.axis_index("tile"), lax.axis_index("pair")
    group = 2 * chips
    core = lax.rem(p, 2)
    above, below = (lax.rem(t + 1, tiles), p), (lax.rem(t + tiles - 1, tiles), p)
    right, left = (t, lax.rem(p + 2, group)), (t, lax.rem(p + group - 2, group))
    other = (t, p + 1 - 2 * core)

    turned_below = lax.rem(t, LINE) == 0
    turned_above = lax.rem(lax.rem(t + 1, tiles), LINE) == 0
    first_core = core == 0

    lead = jnp.where(turned_above, LAST, FIRST)
    ends = {
        "p": (lead, jnp.where(turned_above, FROM_BELOW, FROM_ABOVE), turned_above),
        "q": (LAST + FIRST - lead, jnp.where(turned_above, FROM_ABOVE, FROM_BELOW), jnp.logical_not(turned_above)),
    }
    part_slots = {"p": pl.ds(ends["p"][0], 2), "q": pl.ds(ends["q"][0], 2), "i": INNER, "c": slice(0, 2), "d": slice(2, 4)}

    def greet(sem, device):
        pl.semaphore_signal(sem, inc=1, device_id=device, device_id_type=MESH)

    barrier = pltpu.get_barrier_semaphore()
    greet(barrier, right)
    greet(barrier, left)
    pl.when(jnp.logical_not(first_core))(lambda: greet(barrier, other))
    pl.when(jnp.logical_not(turned_above))(lambda: greet(barrier, above))
    pl.when(turned_below)(lambda: greet(barrier, below))
    fills = {}
    for k, (part, lo, hi) in enumerate((("p", 6, 8), ("p", 0, 2), ("i", 2, 6))):
        at = (LAST, FIRST, INNER.start)[k]
        fill = pltpu.make_async_copy(samples_ref.at[lo:hi], mine[0].at[at : at + hi - lo], local_sem.at[k])
        fill.start()
        fills.setdefault(part, []).append(fill)
    scalars = [
        pltpu.make_async_copy(pairs_ref, pairs, local_sem.at[3]),
        pltpu.make_async_copy(bins_ref, bins, local_sem.at[4]),
    ]
    for copy in scalars:
        copy.start()

    pl.semaphore_wait(
        barrier,
        2 + first_core.astype(jnp.int32) + turned_above.astype(jnp.int32)
        + jnp.logical_not(turned_below).astype(jnp.int32),
    )

    def run(order):
        count = [0]
        sent = []

        def send(src, dst, device):
            k = count[0]
            count[0] += 1
            copy = pltpu.make_async_remote_copy(
                src_ref=src, dst_ref=dst, send_sem=send_sem.at[k], recv_sem=recv_sem.at[k],
                device_id=device, device_id_type=MESH,
            )
            copy.start()
            sent.append(copy)
            return copy

        ring = {}
        cross = {c: [] for c in range(chunks)}
        later = {"s": [], "u": [], "v": []}
        opened = set()

        def forward(step, part, k):
            here = of_step(step)[k] if step else 0
            there = of_step(step + 1)[k]
            cut = (slice(0, half), slice(half, rows))[k] if step + 1 == steps else slice(0, rows)
            slots = part_slots[part]
            return send(mine[here].at[slots, cut], mine[there].at[slots], (right, left)[k])

        def halo(chunk, part):
            own, slots, up = ends[part]
            way = 1 - up.astype(jnp.int32)
            to = lax.rem(t + jnp.where(up, 1, tiles - 1), tiles)
            return pltpu.make_async_remote_copy(
                src_ref=mine[chunk].at[pl.ds(own, 2)], dst_ref=mine[chunk].at[pl.ds(slots, 2)],
                send_sem=halo_send.at[chunk, way], recv_sem=halo_recv.at[chunk, way],
                device_id=(to, p), device_id_type=MESH,
            )

        def halos_here(chunk, act):
            for way, (own, slots, device) in enumerate(((LAST, FROM_BELOW, above), (FIRST, FROM_ABOVE, below))):
                act(
                    pltpu.make_async_remote_copy(
                        src_ref=mine[chunk].at[own : own + 2], dst_ref=mine[chunk].at[slots : slots + 2],
                        send_sem=halo_send.at[chunk, way], recv_sem=halo_recv.at[chunk, way],
                        device_id=device, device_id_type=MESH,
                    )
                )

        def across(chunk, slots):
            if "s" in opened:
                cross[chunk].append(send(mine[chunk].at[slots], theirs[chunk].at[slots], other))
            else:
                later["s"].append((chunk, slots))

        def arrive(part, step):
            if step == 0:
                for fill in fills.get("i" if part == "c" else part, ()):
                    fill.wait()
            ring[step, part] = []
            for k in range(2):
                if step > 0:
                    ring[step - 1, part][k].wait_recv()
                if step < steps:
                    ring[step, part].append(forward(step, part, k))
            for chunk in of_step(step):
                if part == "p":
                    if "v" in opened:
                        halo(chunk, part).start()
                    else:
                        pl.when(jnp.logical_not(turned_below))(lambda: halo(chunk, part).start())
                        later["v"].append(chunk)
                elif part == "q":
                    if "u" in opened:
                        halo(chunk, part).start()
                    else:
                        later["u"].append(chunk)
                    across(chunk, ENDS)
                else:
                    across(chunk, part_slots[part])

        def open_gate(gate):
            opened.add(gate)
            if gate == "s":
                pl.when(jnp.logical_not(first_core))(lambda: pl.semaphore_wait(ready_sem.at[0], 1))
                for chunk, slots in later["s"]:
                    across(chunk, slots)
            elif gate == "u":
                pl.when(jnp.logical_not(turned_above))(lambda: pl.semaphore_wait(ready_sem.at[1], 1))
                for chunk in later["u"]:
                    halo(chunk, "q").start()
            else:

                @pl.when(turned_below)
                def _():
                    pl.semaphore_wait(ready_sem.at[2], 1)
                    for chunk in later["v"]:
                        halo(chunk, "p").start()

        start, band = t * 8, tiles * 8

        def load(step, put, cores):
            for q in range(per_device):
                for side in range(2):
                    slot = slot_of(pairs[side, p * per_device + q], start, band)
                    row = 0
                    for n, core_chunks in enumerate((mine, theirs)):
                        for chunk in of_step(step):
                            held = core_chunks[chunk]
                            if n in cores:
                                put(q, side, row, held[slot].astype(jnp.float32))
                            row += held.shape[1]

        def work(step, cores=(0, 1)):
            if 1 in cores:
                for chunk in of_step(step):
                    for copy in cross[chunk]:
                        copy.wait_recv()
            depth = sum(2 * mine[chunk].shape[1] for chunk in of_step(step))
            if step == 0:
                for copy in scalars:
                    copy.wait()
                for q in range(per_device):
                    weight = 1.0 - jnp.full((1, pixels), bins[0, q], jnp.int32).astype(jnp.float32) / NBINS
                    factor_ref[q] = weight / jnp.float32(rows * group - 1)
                totals = {}

                def add(q, side, row, values):
                    total = jnp.sum(values, axis=0, keepdims=True)
                    totals[q, side] = total if row == 0 else totals[q, side] + total

                load(0, add, cores)
                for (q, side), total in totals.items():
                    shift_ref[2 * q + side] = (total * (1.0 / depth)).astype(jnp.bfloat16).astype(jnp.float32)
            final = step not in early
            into = last_ref if final else u_ref
            before = [n for n in range(step) if (n in early) == (not final)]
            first_row = sum(2 * mine[chunk].shape[1] for n in before for chunk in of_step(n))
            sums = {}

            def put(q, side, row, values):
                u = (values - shift_ref[2 * q + side]).astype(jnp.bfloat16)
                into[2 * q + side, pl.ds(first_row + row, values.shape[0]), :] = u
                total = jnp.sum(u.astype(jnp.float32), axis=0, keepdims=True)
                sums[q, side] = sums[q, side] + total if (q, side) in sums else total

            load(step, put, cores)
            for (q, side), total in sums.items():
                k = 2 * q + side
                total = total if step == 0 else sum_ref[k] + total
                if step < steps or 1 not in cores:
                    sum_ref[k] = total
                else:
                    total = total * (-1.0 / (rows * group)) if side == 0 else total
                    high = total.astype(jnp.bfloat16).astype(jnp.float32)
                    middle = (total - high).astype(jnp.bfloat16).astype(jnp.float32)
                    low = total - high - middle
                    row = lax.broadcasted_iota(jnp.int32, (SPLIT_ROWS, pixels), 0)
                    is_middle = (row == 5) | (row == (2 if side == 0 else 1))
                    is_low = row == (4 if side == 0 else 3)
                    parts = jnp.where(row > 5, 0.0, jnp.where(is_middle, middle, jnp.where(is_low, low, high)))
                    into[k, pl.ds(first_row + depth, SPLIT_ROWS), :] = parts.astype(jnp.bfloat16)

        state = [0, 0]

        def drain():
            done, mark = state
            for copy in sent[done:mark]:
                copy.wait_send()
            state[:] = mark, len(sent)

        def drain_halos(step):
            for chunk in of_step(step):
                halos_here(chunk, lambda copy: copy.wait_send())

        def product(which, piece):
            cut = sum(2 * mine[chunk].shape[1] for n in early[:2] for chunk in of_step(n))
            from_rows = slice(0, cut) if which == "A" else slice(cut, u_ref.shape[1])
            block = per_device * pixels // PIECES
            q, m = divmod(piece * block, pixels)
            gram = lax.dot_general(
                u_ref[2 * q, from_rows, m : m + block], u_ref[2 * q + 1, from_rows, :],
                (((0,), (0,)), ((), ())), preferred_element_type=jnp.float32,
            )
            if which == "A":
                acc_ref[q, m : m + block, :] = gram
            else:
                acc_ref[q, m : m + block, :] += gram

        first = True
        for what, step in order:
            if what in part_slots:
                arrive(what, step)
            elif what == "x":
                for chunk in of_step(step):
                    halos_here(chunk, lambda copy: copy.wait_recv())
                    across(chunk, HALO)
            elif what == "m":
                work(step, (0,))
            elif what == "w":
                work(step, (1,) if step == steps else (0, 1))
            elif what == "y":
                drain()
            elif what == "h":
                drain_halos(step)
            elif what in "AB":
                product(what, step)
            else:
                open_gate(what)
            if first:
                pl.when(first_core)(lambda: greet(ready_sem.at[0], other))
                pl.when(jnp.logical_not(turned_below))(lambda: greet(ready_sem.at[1], below))
                pl.when(turned_above)(lambda: greet(ready_sem.at[2], above))
                first = False
        drain()
        drain()
        drain_halos(steps)

    pl.when(turned_below)(lambda: run(schedule(steps, True)))
    pl.when(jnp.logical_not(turned_below))(lambda: run(schedule(steps, False)))


def finish_kernel(acc_ref, last_ref, factor_ref, out_ref, stage, sem):
    per_device, pixels, _ = acc_ref.shape
    block = min(256, pixels)
    copies = []
    for q in range(per_device):
        for m in range(0, pixels, block):
            rows = slice(m, m + block)
            gram = acc_ref[q, rows, :] + lax.dot_general(
                last_ref[2 * q, :, rows], last_ref[2 * q + 1], (((0,), (0,)), ((), ())),
                preferred_element_type=jnp.float32,
            )
            stage[q, rows, :] = (gram * factor_ref[q]).astype(jnp.bfloat16)
            copy = pltpu.make_async_copy(stage.at[q, rows], out_ref.at[q, rows], sem.at[len(copies)])
            copy.start()
            copies.append(copy)
    for copy in copies:
        copy.wait()


def local(tiles, group, samples, pair_list, taper_bins):
    own_tiles, rows, pixels = samples.shape
    chips = group // 2
    steps = chips // 2
    per_device = taper_bins.shape[0]
    plan = (tiles, chips, steps, rows, pixels, per_device)
    chunk_rows = [rows] * (2 * steps - 1) + [rows // 2] * 2
    chunks = [pltpu.VMEM((SLOTS, r, pixels), jnp.bfloat16) for r in chunk_rows]
    n_copies = 2 * 4 * steps + 4 * len(chunks)
    early = list(range(steps - 1))
    early_rows = sum(2 * rows * (1 if n == 0 else 2) for n in early)
    last_rows = 2 * rows * chips - early_rows + SPLIT_ROWS
    acc, last, factor = pl.pallas_call(
        functools.partial(gather_kernel, plan, early),
        out_shape=(
            pltpu.VMEM((per_device, pixels, pixels), jnp.float32),
            pltpu.VMEM((2 * per_device, last_rows, pixels), jnp.bfloat16),
            pltpu.VMEM((per_device, 1, pixels), jnp.float32),
        ),
        in_specs=[pl.BlockSpec(memory_space=pl.ANY)] * 3,
        out_specs=[pl.BlockSpec(memory_space=pltpu.VMEM)] * 3,
        scratch_shapes=[
            *chunks,
            *chunks,
            pltpu.VMEM((2 * per_device, 1, pixels), jnp.float32),
            pltpu.VMEM((2 * per_device, early_rows, pixels), jnp.bfloat16),
            pltpu.VMEM((2 * per_device, 1, pixels), jnp.float32),
            pltpu.SMEM((2, pair_list.shape[0]), jnp.int32),
            pltpu.SMEM((1, per_device), jnp.int32),
            pltpu.SemaphoreType.DMA((n_copies,)),
            pltpu.SemaphoreType.DMA((n_copies,)),
            pltpu.SemaphoreType.DMA((len(chunks), 2)),
            pltpu.SemaphoreType.DMA((len(chunks), 2)),
            pltpu.SemaphoreType.DMA((5,)),
            pltpu.SemaphoreType.REGULAR((3,)),
        ],
        compiler_params=pltpu.CompilerParams(
            collective_id=0, has_side_effects=True, vmem_limit_bytes=36 * 2**20
        ),
        name="gather_and_sum",
    )(*(pltpu.with_memory_space_constraint(v, pltpu.HBM) for v in (pair_list.T, taper_bins.reshape(1, -1), samples)))
    return pl.pallas_call(
        finish_kernel,
        out_shape=jax.ShapeDtypeStruct((per_device, pixels, pixels), jnp.bfloat16),
        in_specs=[pl.BlockSpec(memory_space=pltpu.VMEM)] * 3,
        out_specs=pl.BlockSpec(memory_space=pl.ANY),
        scratch_shapes=[
            pltpu.VMEM((per_device, pixels, pixels), jnp.bfloat16),
            pltpu.SemaphoreType.DMA((per_device * max(1, pixels // 256),)),
        ],
        compiler_params=pltpu.CompilerParams(vmem_limit_bytes=36 * 2**20),
        name="finish",
    )(acc, last, factor)


def solution(mesh):
    in_specs = (P("tile", "pair", None), P("tile", None), P(("tile", "pair")))
    out_specs = P(("tile", "pair"), None, None)
    body = functools.partial(local, mesh.shape["tile"], mesh.shape["pair"])
    return jax.shard_map(body, mesh=mesh, in_specs=in_specs, out_specs=out_specs, check_vma=False)
```
